128 devices in a mesh: grp: 4 (over x), mem: 32 (over y, z, core).
Axes of the slice: x: 4, y: 4, z: 4, core: 2. Of those that a mesh axis runs over, the one named last changes fastest.
Arguments:
- vectors: float32 [131072, 768], P(('grp', 'mem')), may hold values from -6 to 6
- boundary: float32 [8192, 768], P(('grp', 'mem')), may hold values from -6 to 6
- centroids: float32 [32768, 768], P(('grp', 'mem')), may hold values from -3 to 3
- list_owner: int32 [8192, 8], P(('grp', 'mem')), may hold values from 0 to 127, all different within a row; in each aligned block of 64 rows (0 to 63, 64 to 127, ...) at most 8 rows name the same one
- list_slot: int32 [8192, 8], P(('grp', 'mem')), may hold values from 0 to 255
Outputs:
- resident_score: bfloat16 [131072, 8192], P(('grp', 'mem'))
- posting_residual: float32 [131072, 768], P(('grp', 'mem'))
- posting_dist: float32 [128, 1024], P(('grp', 'mem'))
The draws below stay inside these ranges and needn't reach their ends.
Inputs may be any that keep to these rules, and one draw needn't show every extreme that they name: `list_owner`: A row names 8 different owners. Among the rows of one device no owner is named by more than 8 rows, a bound that some block reaches.
All inputs are finite; a program needn't handle non-finite values.
Results may differ from the reference program's by a relative error of at most 0.006.
Values may be sent and summed in bfloat16 or wider, within the bound.
A program may use at most 192 MiB of HBM per device.

```python
import math
import jax
import jax.numpy as jnp
import numpy as np
from jax import lax

D = 768
CEN_DEV = 256
LIST = 8
V_DEV = 1024
BROWS = 64
PANEL = 8192
CENTROIDS = 32768
VECTORS = 131072
CAP = 8
N_GRP = 4
N_MEM = 32
DEVICES = 128


def set_ends(result, own_key, least, largest):
    extent = result.shape
    spot = [jax.random.randint(jax.random.fold_in(own_key, axis), (), 0, extent[axis]) for axis in range(len(extent))]
    result = result.at[tuple(spot)].set(least)
    longest = extent.index(max(extent))
    spot[longest] = (spot[longest] + 1) % extent[longest]
    return result.at[tuple(spot)].set(largest)


def level_of(key, extent, shards, least, high):
    gain, own = 1.0, jax.random.fold_in(key, 6)
    for axis_at, parts in shards:
        steps = jnp.exp(jax.random.uniform(jax.random.fold_in(own, axis_at), (parts,), jnp.float32, least / len(shards), high / len(shards)))
        gain = gain * jnp.repeat(steps, extent[axis_at] // parts).reshape([-1 if axis == axis_at else 1 for axis in range(len(extent))])
    return gain


def deal_out(stream_key, own, number, rows, count, top, most, slope):
    ranking = jax.random.permutation(stream_key, count)
    crowded, common = shares(count, rows * top, most, slope, True), shares(count, rows * top, most, slope, False)
    places = jnp.arange(count)

    def named(sizes, offset_by):
        used = int((sizes > 0).sum())
        fixed = max(1, used // 4)
        passed = fixed + (places - fixed + offset_by * (used - fixed)) % max(1, count - fixed)
        return jnp.zeros((count,), jnp.int32).at[ranking[jnp.where(places < fixed, places, passed)]].set(jnp.asarray(sizes, jnp.int32))

    sizes = jnp.where(number % 4 == 0, named(crowded, number // 4), named(common, number - number // 4 - 1))
    mixed = jax.random.permutation(jax.random.fold_in(own, 3), count)
    giver, taker = mixed[0:count // 2 * 2:2], mixed[1:count // 2 * 2:2]
    margin = jnp.minimum(sizes[giver] - 1, most - sizes[taker]) // 2
    margin = jnp.where((giver == ranking[0]) | (taker == ranking[0]) | (sizes[taker] == 0), 0, jnp.maximum(margin, 0))
    passed = jax.random.randint(jax.random.fold_in(own, 4), (count // 2,), 0, 1 << 20) % (margin + 1)
    sizes = sizes.at[giver].add(-passed).at[taker].add(passed)
    members = jnp.searchsorted(jnp.cumsum(sizes), jnp.arange(rows * top), side="right").astype(jnp.int32)
    grid = members.reshape(top, rows).T
    grid = grid[jax.random.permutation(jax.random.fold_in(own, 1), rows)]
    offset_by = jax.random.randint(jax.random.fold_in(own, 2), (rows, 1), 0, top)
    return jnp.take_along_axis(grid, (jnp.arange(top)[None, :] + offset_by) % top, axis=1)


def shares(amount, total, limit, slope, full):
    loads = [(1 << 20) // math.isqrt(grade ** slope) + 1 for grade in range(1, amount + 1)]
    largest = limit if full else min(limit, max(-(-total // amount), total * loads[0] // sum(loads)))
    least = 1 if total - largest >= amount - 1 else 0
    given, spare = [largest] + [least] * (amount - 1), total - largest - least * (amount - 1)
    while spare > 0:
        free = [i for i in range(1, amount) if given[i] < largest] or [i for i in range(1, amount) if given[i] < limit]
        mass, budget = sum([loads[i] for i in free]), spare
        for i in free:
            more = min(limit - given[i], max(1, budget * loads[i] // mass), spare)
            given[i] = given[i] + more
            spare = spare - more
    return np.array(given)


def centred(key, shape, deviation, limit, split=(), kind=jnp.bfloat16):
    level = level_of(key, shape, split, -0.22, 0.18) if split else 1.0
    drawn = jax.random.normal(key, shape, jnp.float32) * deviation * level
    return jnp.minimum(jnp.maximum(drawn, -limit), limit).astype(kind)


def setup_inputs(seed: int = 0) -> dict:
    key_of = jax.random.split(jax.random.key(seed), 6)
    vectors = centred(key_of[0], (VECTORS, D), 1.0, 6.0, ((0, 128),), jnp.float32)
    boundary = centred(key_of[1], (DEVICES * BROWS, D), 1.0, 6.0, ((0, 128),), jnp.float32)
    centroids = centred(key_of[2], (CENTROIDS, D), 0.5, 3.0, ((0, 128),), jnp.float32)
    list_owner_keys = jax.random.split(jax.random.fold_in(key_of[3], 1), (DEVICES * BROWS) // BROWS)
    list_owner_turns = jax.random.permutation(jax.random.fold_in(key_of[3], 3), (DEVICES * BROWS) // BROWS)
    list_owner = jax.vmap(lambda own, number: deal_out(jax.random.fold_in(key_of[3], 2), own, number, BROWS, DEVICES, LIST, CAP, 2))(list_owner_keys, list_owner_turns).reshape((DEVICES * BROWS, LIST))
    list_slot = set_ends(jax.random.randint(key_of[4], (DEVICES * BROWS, LIST), 0, CEN_DEV), jax.random.fold_in(key_of[4], 1), 0, CEN_DEV - 1).astype(jnp.int32)
    return {"vectors": vectors, "boundary": boundary, "centroids": centroids, "list_owner": list_owner, "list_slot": list_slot}


def reference(vectors, boundary, centroids, list_owner, list_slot):
    devices = N_GRP * N_MEM
    cen_bf = centroids.astype(jnp.bfloat16)
    cen_norm = lax.optimization_barrier(jnp.sum(centroids * centroids, axis=1))
    vec_bf = vectors.astype(jnp.bfloat16).reshape(devices, V_DEV, D)
    factor = 1.0 / math.sqrt(D)

    def device_scores(device):
        group = device // N_MEM
        start = (group * PANEL).astype(jnp.int32)
        panel_rows = lax.dynamic_slice_in_dim(cen_bf, start, PANEL, 0)
        panel_norms = lax.dynamic_slice_in_dim(cen_norm, start, PANEL, 0)
        resident = lax.dynamic_index_in_dim(vec_bf, device, 0, keepdims=False)
        products = lax.dot_general(resident, panel_rows, (((1,), (1,)), ((), ())), preferred_element_type=jnp.float32)
        return ((2.0 * products - panel_norms[None, :]) * factor).astype(jnp.bfloat16)
    scores = lax.map(device_scores, jnp.arange(devices, dtype=jnp.int32))
    resident_score = scores.reshape(devices * V_DEV, PANEL)
    pairs = BROWS * LIST
    owners = list_owner.reshape(devices, pairs)
    onehot = (owners[:, :, None] == jnp.arange(devices, dtype=jnp.int32)[None, None, :]).astype(jnp.int32)
    before = jnp.cumsum(onehot, axis=1) - onehot
    places = lax.optimization_barrier(jnp.sum(before * onehot, axis=2))
    source = jnp.arange(devices, dtype=jnp.int32)[:, None]
    target = ((owners * devices + source) * CAP + places).reshape(-1)
    sent_rows = jnp.repeat(boundary, LIST, axis=0)
    cluster = (list_owner * CEN_DEV + list_slot).reshape(-1)
    residual = sent_rows - centroids[cluster]
    distance = lax.optimization_barrier(jnp.sum(residual * residual, axis=1)) / D
    posting_residual = jnp.zeros((devices * devices * CAP, D), jnp.float32).at[target].set(residual)
    posting_dist = jnp.zeros((devices * devices * CAP,), jnp.float32).at[target].set(distance)
    return (resident_score, posting_residual, posting_dist.reshape(devices, devices * CAP))
```

```python
import functools
import math

import jax
import jax.numpy as jnp
from jax import lax
from jax.experimental import pallas as pl
from jax.experimental.pallas import tpu as pltpu
from jax.sharding import PartitionSpec as P

D = 768
LIST = 8
CAP = 8
BROWS = 64
CEN = 256
V_DEV = 1024
N_GRP = 4
N_MEM = 32
RING = 4
CHIPS = 16
DEVICES = 128
WIDE = D + 128
FIELD = 512
MESH = pl.DeviceIdType.MESH
FACTOR = 1.0 / math.sqrt(D)
LATER = 4
LAG = 2

ORDER = (
    (0, 0), (3, 0), (1, 0), (0, 3), (0, 1), (2, 0), (3, 3), (3, 1),
    (1, 3), (1, 1), (0, 2), (2, 3), (2, 1), (3, 2), (1, 2), (2, 2),
)
PLACE = {offset: e for e, offset in enumerate(ORDER)}


def sends_of(e):
    da, db = ORDER[e]
    out = []
    if db == 0:
        if da == 0:
            out += [("a", 1, None, PLACE[3, 0]), ("a", 3, None, PLACE[1, 0])]
        elif da == 3:
            out += [("a", 1, 0, PLACE[2, 0])]
        elif da == 1:
            out += [("a", 3, 1, PLACE[2, 0])]
        out += [("b", 1, None, PLACE[da, 3]), ("b", 3, None, PLACE[da, 1])]
    elif db == 3:
        out += [("b", 1, 0, PLACE[da, 2])]
    elif db == 1:
        out += [("b", 3, 1, PLACE[da, 2])]
    return out + [("core", 0, None, e)]


SENDS = [sends_of(e) for e in range(CHIPS)]
FIRST = [sum(len(s) for s in SENDS[:e]) for e in range(CHIPS)]
N_SENDS = sum(len(s) for s in SENDS)


def split(order):
    da, db = ORDER[order]
    return db == 2 or (db == 0 and da == 2)


def position():
    m = lax.axis_index("mem")
    return lax.axis_index("grp"), m // 8, (m // 2) % RING, m % 2


def member(y, z, core, da, db):
    dy = (1 - core) * da + core * db
    dz = (1 - core) * db + core * da
    return (((y + dy) % RING) * RING + (z + dz) % RING) * 2 + core


def offsets(e):
    da = sum(jnp.where(e == k, o[0], 0) for k, o in enumerate(ORDER))
    db = sum(jnp.where(e == k, o[1], 0) for k, o in enumerate(ORDER))
    return da, db


class Stream:
    def __init__(self, buffer, halves, send, recv, recv_core, where):
        self.buffer, self.halves = buffer, halves
        self.send, self.recv, self.recv_core = send, recv, recv_core
        self.x, self.y, self.z, self.core = where

    def block(self, e, half):
        da, db = ORDER[e]
        ref = self.buffer.at[member(self.y, self.z, self.core, da, db)]
        if half is None or not self.halves:
            return ref
        rows = self.buffer.shape[1] // 2
        return ref.at[pl.ds(half * rows, rows)]

    def copies(self, e):
        out = []
        for i, (axis, step, half, there) in enumerate(SENDS[e]):
            if half == 1 and not self.halves:
                continue
            if axis == "core":
                target, sem = member(self.y, self.z, self.core, 0, 0), self.recv_core.at[e]
                target = target + 1 - 2 * self.core
            else:
                da, db = (step, 0) if axis == "a" else (0, step)
                target = member(self.y, self.z, self.core, da, db)
                sem = self.recv.at[there, half or 0]
            ref = self.block(e, half)
            out.append(
                pltpu.make_async_remote_copy(
                    src_ref=ref,
                    dst_ref=ref,
                    send_sem=self.send.at[FIRST[e] + i],
                    recv_sem=sem,
                    device_id=(self.x, target),
                    device_id_type=MESH,
                )
            )
        return out

    def await_block(self, e):
        if e == 0:
            return
        for half in (0, 1) if split(e) and self.halves else (None,):
            ref = self.block(e, half)
            pltpu.make_async_remote_copy(
                src_ref=ref,
                dst_ref=ref,
                send_sem=self.send.at[0],
                recv_sem=self.recv.at[e, half or 0],
                device_id=(self.x, member(self.y, self.z, self.core, 0, 1)),
                device_id_type=MESH,
            ).wait_recv()

    def await_core(self, e, block):
        ref = self.buffer.at[block]
        pltpu.make_async_remote_copy(
            src_ref=ref,
            dst_ref=ref,
            send_sem=self.send.at[0],
            recv_sem=self.recv_core.at[e],
            device_id=(self.x, member(self.y, self.z, 1 - self.core, 0, 0)),
            device_id_type=MESH,
        ).wait_recv()

    def pass_on(self, e):
        for copy in self.copies(e):
            copy.start()

    def await_sends(self):
        for e in range(CHIPS):
            for copy in self.copies(e):
                copy.wait_send()


def norm_row(meta, block):
    return jnp.concatenate([meta[block, 0:1, 128:256], meta[block, 1:2, 128:256]], axis=1)


def scores_of(vec, rows, norm):
    products = lax.dot_general(
        vec, rows, (((1,), (1,)), ((), ())), preferred_element_type=jnp.float32
    )
    return ((2.0 * products - norm) * FACTOR).astype(jnp.bfloat16)


TILE = 256


def gather_kernel(
    vectors, boundary, centroids, pairs,
    scores, cen, meta, vec_bf, arrived,
    bnd, parts, staged,
    vec_sem,
    bnd_send, bnd_recv, bnd_core,
    meta_send, meta_recv, meta_core,
    cen_send, cen_recv, cen_core,
    x_send, x_recv, own_sem,
):
    where = position()
    x, y, z, core = where
    me = member(y, z, core, 0, 0)
    other = 1 - core

    barrier = pltpu.get_barrier_semaphore()
    greeted = [(x, member(y, z, core, da, db)) for da, db in ((1, 0), (3, 0), (0, 1), (0, 3))]
    greeted += [(x, member(y, z, other, 0, 0))]
    greeted += [((x + dx) % N_GRP, me) for dx in (1, 2, 3)]
    for device in greeted:
        pl.semaphore_signal(barrier, inc=1, device_id=device, device_id_type=MESH)

    fetch = pltpu.make_async_copy(vectors, staged, vec_sem)
    fetch.start()

    bnd[me] = boundary[...].astype(jnp.bfloat16)
    packed = pairs[...]
    owner, slot = packed // CEN, packed % CEN
    device_row = lax.broadcasted_iota(jnp.int32, (DEVICES, 128), 0)
    named = [device_row == owner[k : k + 1, :] for k in range(LIST)]
    marks = sum(jnp.where(n, 1.0, 0.0) for n in named)
    before = lax.broadcasted_iota(jnp.int32, (128, 128), 0)
    column = lax.broadcasted_iota(jnp.int32, (128, 128), 1)
    earlier = jnp.where(before < column % BROWS, 1.0, 0.0).astype(jnp.bfloat16)
    counts = jnp.dot(marks.astype(jnp.bfloat16), earlier, preferred_element_type=jnp.float32)
    places = jnp.concatenate(
        [jnp.sum(jnp.where(n, counts, 0.0), axis=0, keepdims=True) for n in named], axis=0
    )
    code = (owner.astype(jnp.float32) * CAP + places) * FIELD + (slot + 1).astype(jnp.float32)
    lane = lax.broadcasted_iota(jnp.int32, (LIST, 128), 1)
    row = lax.broadcasted_iota(jnp.int32, (LIST, 128), 0)
    meta[me, :, 0:128] = jnp.where(lane // BROWS == core, code, 0.0)

    own = centroids[...]
    cen[me] = own.astype(jnp.bfloat16)
    squares = own * own
    partial = sum(squares[:, i * 128 : (i + 1) * 128] for i in range(D // 128))
    norms = [jnp.sum(partial[i * 128 : (i + 1) * 128].T, axis=0, keepdims=True) for i in range(2)]
    meta[me, :, 128:256] = jnp.where(row == 0, norms[0], jnp.where(row == 1, norms[1], 0.0))

    s_bnd = Stream(bnd, True, bnd_send, bnd_recv, bnd_core, where)
    s_meta = Stream(meta, False, meta_send, meta_recv, meta_core, where)
    s_cen = Stream(cen, True, cen_send, cen_recv, cen_core, where)

    pl.semaphore_wait(barrier, len(greeted))
    s_meta.pass_on(0)
    s_bnd.pass_on(0)
    s_cen.pass_on(0)

    fetch.wait()

    @pl.loop(0, V_DEV // 128)
    def _(t):
        rows = pl.ds(pl.multiple_of(t * 128, 128), 128)
        vec_bf[rows, :] = staged[rows, :].astype(jnp.bfloat16)

    for e in range(1, CHIPS):
        s_meta.await_block(e)
        s_meta.pass_on(e)
        s_bnd.await_block(e)
        s_bnd.pass_on(e)

    @pl.loop(0, CHIPS)
    def _(e):
        da, db = offsets(e)
        block = member(y, z, other, da, db)
        s_meta.await_core(e, block)
        s_bnd.await_core(e, block)

    srow = lax.broadcasted_iota(jnp.int32, (N_GRP * 16, 128), 0)
    scol = lax.broadcasted_iota(jnp.int32, (N_GRP * 16, 128), 1)
    wanted = ((srow // 16) * N_MEM + me) * CAP + srow % CAP
    wanted = jnp.where((srow // CAP) % 2 == scol // BROWS, wanted * FIELD, -(1 << 22))
    wanted = wanted.astype(jnp.float32)
    ones = jnp.ones((128, 128), jnp.bfloat16)

    @pl.loop(0, CHIPS)
    def _(p):
        both = meta[2 * p, :, 0:128] + meta[2 * p + 1, :, 0:128]
        found = jnp.zeros((N_GRP * 16, 128), jnp.float32)
        for k in range(LIST):
            apart = both[k : k + 1, :] - wanted
            found += jnp.where((apart > 0.0) & (apart < FIELD), apart, 0.0)
        pick = jnp.where(found > 0.0, 1.0, 0.0).astype(jnp.bfloat16)
        source = bnd[pl.ds(2 * p, 2)].reshape(128, D)
        rows = jnp.dot(pick, source, preferred_element_type=jnp.float32).astype(jnp.bfloat16)
        slots = jnp.dot(found.astype(jnp.bfloat16), ones, preferred_element_type=jnp.float32)
        slots = slots.astype(jnp.bfloat16)
        for g in range(N_GRP):
            parts[g, p, :, 0:D] = rows[g * 16 : (g + 1) * 16]
            parts[g, p, :, D:WIDE] = slots[g * 16 : (g + 1) * 16]

    def across(dx):
        return pltpu.make_async_remote_copy(
            src_ref=parts.at[(x + dx) % N_GRP],
            dst_ref=arrived.at[x],
            send_sem=x_send.at[dx],
            recv_sem=x_recv.at[dx],
            device_id=((x + dx) % N_GRP, me),
            device_id_type=MESH,
        )

    for dx in (2, 1, 3):
        across(dx).start()
    keep = pltpu.make_async_copy(parts.at[x], arrived.at[x], own_sem)
    keep.start()

    def score(block):
        norm = norm_row(meta, block)

        @pl.loop(0, V_DEV // TILE)
        def _(t):
            rows = pl.ds(pl.multiple_of(t * TILE, TILE), TILE)
            scores[block, rows, :] = scores_of(vec_bf[rows, :], cen[block], norm)

    @pl.loop(0, CHIPS + LAG)
    def _(i):
        for e in range(1, CHIPS):

            @pl.when(i == e)
            def _(e=e):
                s_cen.await_block(e)
                s_cen.pass_on(e)

        @pl.when(i < CHIPS - LATER)
        def _():
            da, db = offsets(i)
            score(member(y, z, core, da, db))

        @pl.when(i >= LAG)
        def _():
            e = i - LAG
            da, db = offsets(e)
            block = member(y, z, other, da, db)
            s_cen.await_core(e, block)

            @pl.when(e < CHIPS - LATER)
            def _():
                score(block)

    for dx in (1, 2, 3):
        pltpu.make_async_remote_copy(
            src_ref=parts.at[x],
            dst_ref=arrived.at[(x - dx + N_GRP) % N_GRP],
            send_sem=x_send.at[dx],
            recv_sem=x_recv.at[dx],
            device_id=((x + dx) % N_GRP, me),
            device_id_type=MESH,
        ).wait_recv()
        across(dx).wait_send()
    keep.wait()
    s_meta.await_sends()
    s_bnd.await_sends()
    s_cen.await_sends()


def finish_kernel(
    scores, cen, meta, vec_bf, arrived, centroids,
    scores_out, residual_out, dist,
    late, residual,
    done_sem, late_sem, residual_sem,
):
    x, y, z, core = position()

    def block_of(e, side):
        da, db = offsets(e)
        return member(y, z, (core + side) % 2, da, db)

    def columns(block):
        return scores_out.at[:, pl.ds(pl.multiple_of(block * CEN, CEN), CEN)]

    def early(i):
        block = block_of(i // 2, i % 2)
        return pltpu.make_async_copy(scores.at[block], columns(block), done_sem.at[i])

    n_early, n_late = 2 * (CHIPS - LATER), 2 * LATER

    @pl.loop(0, n_early)
    def _(i):
        early(i).start()

    def late_copy(i):
        block = block_of(CHIPS - LATER + i // 2, i % 2)
        return pltpu.make_async_copy(late.at[i], columns(block), late_sem.at[i])

    @pl.loop(0, n_late)
    def _(i):
        block = block_of(CHIPS - LATER + i // 2, i % 2)
        norm = norm_row(meta, block)

        @pl.loop(0, V_DEV // TILE)
        def _(t):
            rows = pl.ds(pl.multiple_of(t * TILE, TILE), TILE)
            late[i, rows, :] = scores_of(vec_bf[rows, :], cen[block], norm)

        late_copy(i).start()

    own = centroids[...]
    high = own.astype(jnp.bfloat16)
    rest = own - high.astype(jnp.float32)
    middle = rest.astype(jnp.bfloat16)
    low = (rest - middle.astype(jnp.float32)).astype(jnp.bfloat16)
    lane = lax.broadcasted_iota(jnp.int32, (256, 128), 1).astype(jnp.float32)

    def residual_copy(g):
        rows = pl.ds(g * 256, 256)
        return pltpu.make_async_copy(residual.at[rows], residual_out.at[rows], residual_sem.at[g])

    for g in range(N_GRP):
        got = arrived[g].reshape(256, WIDE)
        slot = got[:, D:WIDE].astype(jnp.float32)
        pick = jnp.concatenate(
            [jnp.where(slot == lane + 1.0, 1.0, 0.0), jnp.where(slot == lane + 129.0, 1.0, 0.0)], axis=1
        ).astype(jnp.bfloat16)
        centre = jnp.dot(pick, high, preferred_element_type=jnp.float32) + (
            jnp.dot(pick, middle, preferred_element_type=jnp.float32)
            + jnp.dot(pick, low, preferred_element_type=jnp.float32)
        )
        value = got[:, 0:D].astype(jnp.float32) - centre
        residual[g * 256 : (g + 1) * 256, :] = value
        residual_copy(g).start()
        squares = value * value
        partial = sum(squares[:, i * 128 : (i + 1) * 128] for i in range(D // 128))
        for i in range(2):
            total = jnp.sum(partial[i * 128 : (i + 1) * 128].T, axis=0, keepdims=True)
            dist[:, (2 * g + i) * 128 : (2 * g + i + 1) * 128] = total / D

    @pl.loop(0, n_early)
    def _(i):
        early(i).wait()

    @pl.loop(0, n_late)
    def _(i):
        late_copy(i).wait()

    for g in range(N_GRP):
        residual_copy(g).wait()


def on_device(vectors, boundary, centroids, list_owner, list_slot):
    packed = (list_owner * CEN + list_slot).T
    pairs = jnp.concatenate([packed, packed], axis=1)
    vmem = pl.BlockSpec(memory_space=pltpu.VMEM)
    hbm = pl.BlockSpec(memory_space=pl.ANY)
    dma = pltpu.SemaphoreType.DMA
    stream = [dma((N_SENDS,)), dma((CHIPS, 2)), dma((CHIPS,))]
    scores, cen, meta, vec_bf, arrived = pl.pallas_call(
        gather_kernel,
        out_shape=(
            pltpu.VMEM((N_MEM, V_DEV, CEN), jnp.bfloat16),
            pltpu.VMEM((N_MEM, CEN, D), jnp.bfloat16),
            pltpu.VMEM((N_MEM, LIST, 256), jnp.float32),
            pltpu.VMEM((V_DEV, D), jnp.bfloat16),
            pltpu.VMEM((N_GRP, CHIPS, 16, WIDE), jnp.bfloat16),
        ),
        in_specs=[hbm, vmem, vmem, vmem],
        out_specs=[vmem] * 5,
        scratch_shapes=[
            pltpu.VMEM((N_MEM, BROWS, D), jnp.bfloat16),
            pltpu.VMEM((N_GRP, CHIPS, 16, WIDE), jnp.bfloat16),
            pltpu.VMEM((V_DEV, D), jnp.float32),
            dma,
            *stream,
            *stream,
            *stream,
            dma((N_GRP,)),
            dma((N_GRP,)),
            dma,
        ],
        compiler_params=pltpu.CompilerParams(
            collective_id=0, has_side_effects=True, vmem_limit_bytes=12 << 20
        ),
        name="gather",
    )(vectors, boundary, centroids, pairs)
    return pl.pallas_call(
        finish_kernel,
        out_shape=(
            jax.ShapeDtypeStruct((V_DEV, N_MEM * CEN), jnp.bfloat16),
            jax.ShapeDtypeStruct((DEVICES * CAP, D), jnp.float32),
            jax.ShapeDtypeStruct((1, DEVICES * CAP), jnp.float32),
        ),
        in_specs=[vmem] * 6,
        out_specs=[hbm, hbm, vmem],
        scratch_shapes=[
            pltpu.VMEM((2 * LATER, V_DEV, CEN), jnp.bfloat16),
            pltpu.VMEM((DEVICES * CAP, D), jnp.float32),
            dma((2 * (CHIPS - LATER),)),
            dma((2 * LATER,)),
            dma((N_GRP,)),
        ],
        compiler_params=pltpu.CompilerParams(vmem_limit_bytes=12 << 20),
        name="finish",
    )(scores, cen, meta, vec_bf, arrived, centroids)


def solution(mesh):
    spec = P(("grp", "mem"), None)
    return jax.shard_map(
        on_device,
        mesh=mesh,
        in_specs=(spec,) * 5,
        out_specs=(spec,) * 3,
        check_vma=False,
    )
```

```python
import functools
import math

import jax
import jax.numpy as jnp
from jax import lax
from jax.experimental import pallas as pl
from jax.experimental.pallas import tpu as pltpu
from jax.sharding import PartitionSpec as P

D = 768
LIST = 8
CAP = 8
BROWS = 64
WIDE = D + 128
CEN = 256
V_DEV = 1024
N_GRP = 4
N_MEM = 32
RING = 4
CHIPS = 16
DEVICES = 128
FIELD = 512
MESH = pl.DeviceIdType.MESH
FACTOR = 1.0 / math.sqrt(D)
FIRST_AT, SECOND_AT = 8, 14
ROWS_LAG = 2
LATER = 2
LAG = 2
RESIDUALS_AT = 13

ORDER = (
    (0, 0), (3, 0), (1, 0), (0, 3), (0, 1), (2, 0), (3, 3), (3, 1),
    (1, 3), (1, 1), (0, 2), (2, 3), (2, 1), (3, 2), (1, 2), (2, 2),
)
PLACE = {offset: e for e, offset in enumerate(ORDER)}


def known(e):
    da, db = ORDER[e]
    return max(e, PLACE[db, da])


def sends_of(e):
    da, db = ORDER[e]
    out = []
    if db == 0:
        if da == 0:
            out += [("a", 1, None, PLACE[3, 0]), ("a", 3, None, PLACE[1, 0])]
        elif da == 3:
            out += [("a", 1, 0, PLACE[2, 0])]
        elif da == 1:
            out += [("a", 3, 1, PLACE[2, 0])]
        out += [("b", 1, None, PLACE[da, 3]), ("b", 3, None, PLACE[da, 1])]
    elif db == 3:
        out += [("b", 1, 0, PLACE[da, 2])]
    elif db == 1:
        out += [("b", 3, 1, PLACE[da, 2])]
    return out + [("core", 0, None, e)]


SENDS = [sends_of(e) for e in range(CHIPS)]
FIRST = [sum(len(s) for s in SENDS[:e]) for e in range(CHIPS)]
N_SENDS = sum(len(s) for s in SENDS)


def split(order):
    da, db = ORDER[order]
    return db == 2 or (db == 0 and da == 2)


def position():
    m = lax.axis_index("mem")
    return lax.axis_index("grp"), m // 8, (m // 2) % RING, m % 2


def member(y, z, core, da, db):
    dy = (1 - core) * da + core * db
    dz = (1 - core) * db + core * da
    return (((y + dy) % RING) * RING + (z + dz) % RING) * 2 + core


def offsets(e):
    da = sum(jnp.where(e == k, o[0], 0) for k, o in enumerate(ORDER))
    db = sum(jnp.where(e == k, o[1], 0) for k, o in enumerate(ORDER))
    return da, db


class Stream:
    def __init__(self, buffer, send, recv, recv_core, where):
        self.buffer = buffer
        self.send, self.recv, self.recv_core = send, recv, recv_core
        self.x, self.y, self.z, self.core = where

    def block(self, e, half):
        da, db = ORDER[e]
        ref = self.buffer.at[member(self.y, self.z, self.core, da, db)]
        if half is None:
            return ref
        rows = self.buffer.shape[1] // 2
        return ref.at[pl.ds(half * rows, rows)]

    def copies(self, e, axes=("a", "b", "core")):
        out = []
        for i, (axis, step, half, there) in enumerate(SENDS[e]):
            if axis not in axes:
                continue
            if axis == "core":
                target, sem = member(self.y, self.z, self.core, 0, 0), self.recv_core.at[e]
                target = target + 1 - 2 * self.core
            else:
                da, db = (step, 0) if axis == "a" else (0, step)
                target = member(self.y, self.z, self.core, da, db)
                sem = self.recv.at[there, half or 0]
            ref = self.block(e, half)
            copy = pltpu.make_async_remote_copy(
                src_ref=ref,
                dst_ref=ref,
                send_sem=self.send.at[FIRST[e] + i],
                recv_sem=sem,
                device_id=(self.x, target),
                device_id_type=MESH,
            )
            out.append(copy)
        return out

    def await_block(self, e):
        if e == 0:
            return
        for half in (0, 1) if split(e) else (None,):
            ref = self.block(e, half)
            pltpu.make_async_remote_copy(
                src_ref=ref,
                dst_ref=ref,
                send_sem=self.send.at[0],
                recv_sem=self.recv.at[e, half or 0],
                device_id=(self.x, member(self.y, self.z, self.core, 0, 1)),
                device_id_type=MESH,
            ).wait_recv()

    def await_core(self, e, block):
        ref = self.buffer.at[block]
        pltpu.make_async_remote_copy(
            src_ref=ref,
            dst_ref=ref,
            send_sem=self.send.at[0],
            recv_sem=self.recv_core.at[e],
            device_id=(self.x, member(self.y, self.z, 1 - self.core, 0, 0)),
            device_id_type=MESH,
        ).wait_recv()

    def pass_on(self, e, axes=("a", "b", "core")):
        for copy in self.copies(e, axes):
            copy.start()

    def await_sends(self):
        for e in range(CHIPS):
            for copy in self.copies(e):
                copy.wait_send()


def norm_row(bnd, block):
    part = bnd[block, 16:32, D:WIDE].astype(jnp.float32)
    both = part[8:10] + (part[10:12] + part[12:14])
    return jnp.concatenate([both[0:1], both[1:2]], axis=1)


def scores_of(vec, rows, norm):
    products = lax.dot_general(
        vec, rows, (((1,), (1,)), ((), ())), preferred_element_type=jnp.float32
    )
    return (products * (2.0 * FACTOR) - norm).astype(jnp.bfloat16)


TILE = 1024


def gather_kernel(
    vectors, boundary, centroids, owners, slots,
    scores, cen, bnd, vec_bf, residual, dist,
    parts, arrived, kept, part_slots, arrived_slots, rows_in, centre_in, owners_in, slots_in,
    in_sem,
    bnd_send, bnd_recv, bnd_core,
    cen_send, cen_recv, cen_core,
    x_send, x_recv, own_sem,
):
    where = position()
    x, y, z, core = where
    me = member(y, z, core, 0, 0)
    other = 1 - core

    barrier = pltpu.get_barrier_semaphore()
    greeted = [(x, member(y, z, core, da, db)) for da, db in ((1, 0), (3, 0), (0, 1), (0, 3))]
    greeted += [(x, member(y, z, other, 0, 0))]
    greeted += [((x + dx) % N_GRP, me) for dx in (1, 2, 3)]
    for device in greeted:
        pl.semaphore_signal(barrier, inc=1, device_id=device, device_id_type=MESH)

    fetches = [
        pltpu.make_async_copy(source, target, in_sem.at[i])
        for i, (source, target) in enumerate(
            ((centroids, centre_in), (owners, owners_in), (slots, slots_in), (boundary, rows_in), (vectors, residual))
        )
    ]
    for fetch in fetches:
        fetch.start()

    s_bnd = Stream(bnd, bnd_send, bnd_recv, bnd_core, where)
    s_cen = Stream(cen, cen_send, cen_recv, cen_core, where)

    fetches[0].wait()
    own = centre_in[...]
    cen[me] = own.astype(jnp.bfloat16)
    pl.semaphore_wait(barrier, len(greeted))

    fetches[1].wait()
    fetches[2].wait()
    owner = jnp.concatenate([owners_in[...]] * 2, axis=1)
    slot = jnp.concatenate([slots_in[...]] * 2, axis=1)
    device_row = lax.broadcasted_iota(jnp.int32, (DEVICES, 128), 0)
    named = [device_row == owner[k : k + 1, :] for k in range(LIST)]
    marks = sum(jnp.where(n, 1.0, 0.0) for n in named)
    before = lax.broadcasted_iota(jnp.int32, (128, 128), 0)
    column = lax.broadcasted_iota(jnp.int32, (128, 128), 1)
    earlier = jnp.where(before < column % BROWS, 1.0, 0.0).astype(jnp.bfloat16)
    counts = jnp.dot(marks.astype(jnp.bfloat16), earlier, preferred_element_type=jnp.float32)
    places = jnp.concatenate(
        [jnp.sum(jnp.where(n, counts, 0.0), axis=0, keepdims=True) for n in named], axis=0
    )
    lane = lax.broadcasted_iota(jnp.int32, (LIST, 128), 1)
    lists = [
        jnp.where(lane // BROWS == core, a, 0.0)
        for a in (owner.astype(jnp.float32), places, (slot + 1).astype(jnp.float32))
    ]
    squares = own * own
    partial = sum(squares[:, i * 128 : (i + 1) * 128] for i in range(D // 128))
    norms = [jnp.sum(partial[i * 128 : (i + 1) * 128].T, axis=0, keepdims=True) for i in range(2)]
    norm = jnp.concatenate(norms, axis=0) * FACTOR
    high = norm.astype(jnp.bfloat16).astype(jnp.float32)
    middle = (norm - high).astype(jnp.bfloat16).astype(jnp.float32)
    low = norm - high - middle
    info = [*lists, high, middle, low, jnp.zeros((BROWS - 3 * LIST - 6, 128), jnp.float32)]
    bnd[me, :, D:WIDE] = jnp.concatenate(info, axis=0).astype(jnp.bfloat16)
    fetches[3].wait()
    bnd[me, :, 0:D] = rows_in[...].astype(jnp.bfloat16)

    s_bnd.pass_on(0)

    fetches[4].wait()

    @pl.loop(0, V_DEV // 128)
    def _(t):
        rows = pl.ds(pl.multiple_of(t * 128, 128), 128)
        vec_bf[rows, :] = residual[rows, :].astype(jnp.bfloat16)

    srow = lax.broadcasted_iota(jnp.int32, (N_GRP * 16, 128), 0)
    scol = lax.broadcasted_iota(jnp.int32, (N_GRP * 16, 128), 1)
    wanted = ((srow // 16) * N_MEM + me) * CAP + srow % CAP
    wanted = jnp.where((srow // CAP) % 2 == scol // BROWS, wanted * FIELD, -(1 << 22))
    wanted = wanted.astype(jnp.float32)
    ones = jnp.ones((128, 128), jnp.bfloat16)

    place = lax.broadcasted_iota(jnp.int32, (N_GRP * 16, 128), 1)

    def select(e):
        da, db = ORDER[e]
        p = member(y, z, core, da, db) // 2
        s_bnd.await_core(PLACE[db, da], 2 * p + other)
        info = bnd[2 * p, 0:32, D:WIDE].astype(jnp.float32) + bnd[2 * p + 1, 0:32, D:WIDE].astype(jnp.float32)
        both = (info[0:8] * CAP + info[8:16]) * FIELD + info[16:24]
        found = jnp.zeros((N_GRP * 16, 128), jnp.float32)
        for k in range(LIST):
            apart = both[k : k + 1, :] - wanted
            found += jnp.where((apart > 0.0) & (apart < FIELD), apart, 0.0)
        pick = jnp.where(found > 0.0, 1.0, 0.0).astype(jnp.bfloat16)
        source = bnd[pl.ds(2 * p, 2), :, 0:D].reshape(128, D)
        rows = jnp.dot(pick, source, preferred_element_type=jnp.float32).astype(jnp.bfloat16)
        for g in range(N_GRP):
            parts[g, p] = rows[g * 16 : (g + 1) * 16]
        for dx in (2, 1, 3):
            pltpu.make_async_remote_copy(
                src_ref=parts.at[(x + dx) % N_GRP, p],
                dst_ref=arrived.at[x, p],
                send_sem=x_send.at[dx, 0],
                recv_sem=x_recv.at[dx, 0],
                device_id=((x + dx) % N_GRP, me),
                device_id_type=MESH,
            ).start()
        number = jnp.dot(found.astype(jnp.bfloat16), ones, preferred_element_type=jnp.float32)
        kept[...] += jnp.where(place == p, number, 0.0)

    kept[...] = jnp.zeros_like(kept)
    for step in range(CHIPS + ROWS_LAG):
        if 0 < step < CHIPS:
            s_bnd.await_block(step)
            s_bnd.pass_on(step)
        if step == FIRST_AT:
            s_cen.pass_on(0, ("a", "core"))
        if step == SECOND_AT:
            s_cen.pass_on(0, ("b",))
        for e in range(CHIPS):
            if known(e) == step - ROWS_LAG:
                select(e)
    for g in range(N_GRP):
        part_slots[g] = kept[g * 16 : (g + 1) * 16].astype(jnp.bfloat16)

    def across(dx, i, arriving):
        to = (x + dx) % N_GRP
        origin = (x - dx + N_GRP) % N_GRP if arriving else x
        a, b = ((parts, arrived), (part_slots, arrived_slots))[i]
        return pltpu.make_async_remote_copy(
            src_ref=a.at[to],
            dst_ref=b.at[origin],
            send_sem=x_send.at[dx, i],
            recv_sem=x_recv.at[dx, i],
            device_id=(to, me),
            device_id_type=MESH,
        )

    for dx in (2, 1, 3):
        across(dx, 1, False).start()
    keeps = [
        pltpu.make_async_copy(a.at[x], b.at[x], own_sem.at[i])
        for i, (a, b) in enumerate(((parts, arrived), (part_slots, arrived_slots)))
    ]
    for keep in keeps:
        keep.start()

    def residuals():
        for dx in (1, 2, 3):
            for i in (0, 1):
                across(dx, i, True).wait_recv()
        for keep in keeps:
            keep.wait()
        own = centre_in[...]
        high = own.astype(jnp.bfloat16)
        rest = own - high.astype(jnp.float32)
        middle = rest.astype(jnp.bfloat16)
        low = (rest - middle.astype(jnp.float32)).astype(jnp.bfloat16)
        lane = lax.broadcasted_iota(jnp.int32, (256, 128), 1)
        pair = lax.broadcasted_iota(jnp.int32, (256, 128), 0) // 16
        at = lane.astype(jnp.float32)
        for g in range(N_GRP):
            numbers = jnp.concatenate([arrived_slots[g].astype(jnp.float32)] * CHIPS, axis=0)
            numbers = jnp.where(lane == pair, numbers, 0.0).astype(jnp.bfloat16)
            number = jnp.dot(numbers, ones, preferred_element_type=jnp.float32)
            pick = jnp.concatenate(
                [jnp.where(number == at + 1.0, 1.0, 0.0), jnp.where(number == at + 129.0, 1.0, 0.0)], axis=1
            ).astype(jnp.bfloat16)
            centre = jnp.dot(pick, high, preferred_element_type=jnp.float32) + (
                jnp.dot(pick, middle, preferred_element_type=jnp.float32)
                + jnp.dot(pick, low, preferred_element_type=jnp.float32)
            )
            value = arrived[g].reshape(256, D).astype(jnp.float32) - centre
            residual[g * 256 : (g + 1) * 256, :] = value
            squares = value * value
            partial = sum(squares[:, i * 128 : (i + 1) * 128] for i in range(D // 128))
            for i in range(2):
                total = jnp.sum(partial[i * 128 : (i + 1) * 128].T, axis=0, keepdims=True)
                dist[:, (2 * g + i) * 128 : (2 * g + i + 1) * 128] = total / D

    def score(block):
        norm = norm_row(bnd, block)

        @pl.loop(0, V_DEV // TILE)
        def _(t):
            rows = pl.ds(pl.multiple_of(t * TILE, TILE), TILE)
            scores[block, rows, :] = scores_of(vec_bf[rows, :], cen[block], norm)

    @pl.loop(0, CHIPS + LAG)
    def _(i):
        for e in range(1, CHIPS):

            @pl.when(i == e)
            def _(e=e):
                s_cen.await_block(e)
                s_cen.pass_on(e)

        @pl.when(i == RESIDUALS_AT)
        def _():
            residuals()

        @pl.when(i < CHIPS - LATER)
        def _():
            da, db = offsets(i)
            score(member(y, z, core, da, db))

        @pl.when(i >= LAG)
        def _():
            e = i - LAG
            da, db = offsets(e)
            block = member(y, z, other, da, db)
            s_cen.await_core(e, block)

            @pl.when(e < CHIPS - LATER)
            def _():
                score(block)

    for dx in (1, 2, 3):
        for i in (0, 1):
            across(dx, i, False).wait_send()
    s_bnd.await_sends()
    s_cen.await_sends()


def finish_kernel(
    scores, cen, bnd, vec_bf, residual, dist,
    scores_out, residual_out, dist_out,
    late,
    done_sem, late_sem, residual_sem,
):
    x, y, z, core = position()

    def block_of(e, side):
        da, db = offsets(e)
        return member(y, z, (core + side) % 2, da, db)

    def columns(block):
        return scores_out.at[:, pl.ds(pl.multiple_of(block * CEN, CEN), CEN)]

    def early(i):
        block = block_of(i // 2, i % 2)
        return pltpu.make_async_copy(scores.at[block], columns(block), done_sem.at[i])

    n_early, n_late = 2 * (CHIPS - LATER), 2 * LATER

    @pl.loop(0, n_early)
    def _(i):
        early(i).start()

    rows_copies = [
        pltpu.make_async_copy(residual, residual_out, residual_sem.at[0]),
        pltpu.make_async_copy(dist, dist_out, residual_sem.at[1]),
    ]
    for copy in rows_copies:
        copy.start()

    def late_copy(i):
        block = block_of(CHIPS - LATER + i // 2, i % 2)
        return pltpu.make_async_copy(late.at[i], columns(block), late_sem.at[i])

    @pl.loop(0, n_late)
    def _(i):
        block = block_of(CHIPS - LATER + i // 2, i % 2)
        norm = norm_row(bnd, block)

        @pl.loop(0, V_DEV // TILE)
        def _(t):
            rows = pl.ds(pl.multiple_of(t * TILE, TILE), TILE)
            late[i, rows, :] = scores_of(vec_bf[rows, :], cen[block], norm)

        late_copy(i).start()

    @pl.loop(0, n_early)
    def _(i):
        early(i).wait()

    @pl.loop(0, n_late)
    def _(i):
        late_copy(i).wait()

    for copy in rows_copies:
        copy.wait()


def on_device(vectors, boundary, centroids, list_owner, list_slot):
    vmem = pl.BlockSpec(memory_space=pltpu.VMEM)
    hbm = pl.BlockSpec(memory_space=pltpu.HBM)
    dma = pltpu.SemaphoreType.DMA
    stream = [dma((N_SENDS,)), dma((CHIPS, 2)), dma((CHIPS,))]
    arrays = (vectors, boundary, centroids, list_owner.T, list_slot.T)
    scores, cen, bnd, vec_bf, residual, dist = pl.pallas_call(
        gather_kernel,
        out_shape=(
            pltpu.VMEM((N_MEM, V_DEV, CEN), jnp.bfloat16),
            pltpu.VMEM((N_MEM, CEN, D), jnp.bfloat16),
            pltpu.VMEM((N_MEM, BROWS, WIDE), jnp.bfloat16),
            pltpu.VMEM((V_DEV, D), jnp.bfloat16),
            pltpu.VMEM((V_DEV, D), jnp.float32),
            pltpu.VMEM((1, DEVICES * CAP), jnp.float32),
        ),
        in_specs=[hbm] * 5,
        out_specs=[vmem] * 6,
        scratch_shapes=[
            pltpu.VMEM((N_GRP, CHIPS, 16, D), jnp.bfloat16),
            pltpu.VMEM((N_GRP, CHIPS, 16, D), jnp.bfloat16),
            pltpu.VMEM((N_GRP * 16, 128), jnp.float32),
            pltpu.VMEM((N_GRP, 16, 128), jnp.bfloat16),
            pltpu.VMEM((N_GRP, 16, 128), jnp.bfloat16),
            pltpu.VMEM((BROWS, D), jnp.float32),
            pltpu.VMEM((CEN, D), jnp.float32),
            pltpu.VMEM((LIST, BROWS), jnp.int32),
            pltpu.VMEM((LIST, BROWS), jnp.int32),
            dma((5,)),
            *stream,
            *stream,
            dma((N_GRP, 2)),
            dma((N_GRP, 2)),
            dma((2,)),
        ],
        compiler_params=pltpu.CompilerParams(
            collective_id=0, has_side_effects=True, vmem_limit_bytes=10 << 20
        ),
        name="gather",
    )(*[pltpu.with_memory_space_constraint(a, pltpu.HBM) for a in arrays])
    return pl.pallas_call(
        finish_kernel,
        out_shape=(
            jax.ShapeDtypeStruct((V_DEV, N_MEM * CEN), jnp.bfloat16),
            jax.ShapeDtypeStruct((DEVICES * CAP, D), jnp.float32),
            jax.ShapeDtypeStruct((1, DEVICES * CAP), jnp.float32),
        ),
        in_specs=[vmem] * 6,
        out_specs=[hbm] * 3,
        scratch_shapes=[
            pltpu.VMEM((2 * LATER, V_DEV, CEN), jnp.bfloat16),
            dma((2 * (CHIPS - LATER),)),
            dma((2 * LATER,)),
            dma((2,)),
        ],
        compiler_params=pltpu.CompilerParams(vmem_limit_bytes=10 << 20),
        name="finish",
    )(scores, cen, bnd, vec_bf, residual, dist)


def solution(mesh):
    spec = P(("grp", "mem"), None)
    return jax.shard_map(
        on_device,
        mesh=mesh,
        in_specs=(spec,) * 5,
        out_specs=(spec,) * 3,
        check_vma=False,
    )
```

```python
import functools
import math

import jax
import jax.numpy as jnp
from jax import lax
from jax.experimental import pallas as pl
from jax.experimental.pallas import tpu as pltpu
from jax.sharding import PartitionSpec as P

D = 768
LIST = 8
CAP = 8
BROWS = 64
WIDE = D + 128
CEN = 256
V_DEV = 1024
N_GRP = 4
N_MEM = 32
RING = 4
CHIPS = 16
DEVICES = 128
FIELD = 512
MESH = pl.DeviceIdType.MESH
FACTOR = 1.0 / math.sqrt(D)
OWN_AT = (("a", 0, 4), ("a", 1, 7), ("b", 0, 10), ("b", 1, 13), ("core", None, 13))
ROWS_LAG = 2
LATER = 4
LAG = 2
RESIDUALS_AT = 13

ORDER = (
    (0, 0), (3, 0), (1, 0), (0, 3), (0, 1), (2, 0), (3, 3), (3, 1),
    (1, 3), (1, 1), (0, 2), (2, 3), (2, 1), (3, 2), (1, 2), (2, 2),
)
PLACE = {offset: e for e, offset in enumerate(ORDER)}


def known(e):
    da, db = ORDER[e]
    return max(e, PLACE[db, da])


def sends_of(e):
    da, db = ORDER[e]
    out = []
    if db == 0:
        if da == 0:
            out += [("a", 1, h, PLACE[3, 0]) for h in (0, 1)] + [("a", 3, h, PLACE[1, 0]) for h in (0, 1)]
        elif da == 3:
            out += [("a", 1, 0, PLACE[2, 0])]
        elif da == 1:
            out += [("a", 3, 1, PLACE[2, 0])]
        for half in (0, 1) if da == 0 else (None,):
            out += [("b", 1, half, PLACE[da, 3]), ("b", 3, half, PLACE[da, 1])]
    elif db == 3:
        out += [("b", 1, 0, PLACE[da, 2])]
    elif db == 1:
        out += [("b", 3, 1, PLACE[da, 2])]
    return out + [("core", 0, None, e)]


SENDS = [sends_of(e) for e in range(CHIPS)]
FIRST = [sum(len(s) for s in SENDS[:e]) for e in range(CHIPS)]
N_SENDS = sum(len(s) for s in SENDS)


def split(order):
    da, db = ORDER[order]
    return db == 2 or (db == 0 and da == 2) or 0 in (da, db) and 2 not in (da, db)


def position():
    m = lax.axis_index("mem")
    return lax.axis_index("grp"), lax.div(m, 8), lax.rem(lax.div(m, 2), RING), lax.rem(m, 2)


def member(y, z, core, da, db):
    dy = (1 - core) * da + core * db
    dz = (1 - core) * db + core * da
    return (lax.rem(y + dy, RING) * RING + lax.rem(z + dz, RING)) * 2 + core


def offsets(e):
    da = sum(jnp.where(e == k, o[0], 0) for k, o in enumerate(ORDER))
    db = sum(jnp.where(e == k, o[1], 0) for k, o in enumerate(ORDER))
    return da, db


class Stream:
    def __init__(self, buffer, send, recv, recv_core, where, ids):
        self.buffer = buffer
        self.send, self.recv, self.recv_core = send, recv, recv_core
        self.x, self.y, self.z, self.core = where
        self.ids = ids

    def block(self, e, half):
        ref = self.buffer.at[self.ids[ORDER[e]]]
        if half is None:
            return ref
        rows = self.buffer.shape[1] // 2
        return ref.at[pl.ds(half * rows, rows)]

    def copies(self, e, axes=("a", "b", "core"), halves=(None, 0, 1)):
        out = []
        for i, (axis, step, half, there) in enumerate(SENDS[e]):
            if axis not in axes or half not in halves:
                continue
            if axis == "core":
                target, sem = self.ids[0, 0] + 1 - 2 * self.core, self.recv_core.at[e]
            else:
                target = self.ids[(step, 0) if axis == "a" else (0, step)]
                sem = self.recv.at[there, half or 0]
            ref = self.block(e, half)
            copy = pltpu.make_async_remote_copy(
                src_ref=ref,
                dst_ref=ref,
                send_sem=self.send.at[FIRST[e] + i],
                recv_sem=sem,
                device_id=(self.x, target),
                device_id_type=MESH,
            )
            out.append(copy)
        return out

    def await_block(self, e):
        if e == 0:
            return
        for half in (0, 1) if split(e) else (None,):
            ref = self.block(e, half)
            pltpu.make_async_remote_copy(
                src_ref=ref,
                dst_ref=ref,
                send_sem=self.send.at[0],
                recv_sem=self.recv.at[e, half or 0],
                device_id=(self.x, self.ids[0, 1]),
                device_id_type=MESH,
            ).wait_recv()

    def await_core(self, e, block):
        ref = self.buffer.at[block]
        pltpu.make_async_remote_copy(
            src_ref=ref,
            dst_ref=ref,
            send_sem=self.send.at[0],
            recv_sem=self.recv_core.at[e],
            device_id=(self.x, self.ids[0, 0] + 1 - 2 * self.core),
            device_id_type=MESH,
        ).wait_recv()

    def pass_on(self, e, axes=("a", "b", "core"), halves=(None, 0, 1)):
        for copy in self.copies(e, axes, halves):
            copy.start()

    def await_sends(self):
        for e in range(CHIPS):
            for copy in self.copies(e):
                copy.wait_send()


def norm_row(bnd, block):
    part = bnd[block, 16:32, D:WIDE].astype(jnp.float32)
    both = part[8:10] + (part[10:12] + part[12:14])
    return jnp.concatenate([both[0:1], both[1:2]], axis=1)


def scores_of(vec, rows, norm):
    products = lax.dot_general(
        vec, rows, (((1,), (1,)), ((), ())), preferred_element_type=jnp.float32
    )
    return (products * (2.0 * FACTOR) - norm).astype(jnp.bfloat16)


TILE = 1024


def gather_kernel(
    vectors, boundary, centroids, owners, slots,
    scores, cen, bnd, vec_bf, residual, dist,
    parts, arrived, kept, part_slots, arrived_slots, rows_in, centre_in, owners_in, slots_in,
    in_sem,
    bnd_send, bnd_recv, bnd_core,
    cen_send, cen_recv, cen_core,
    x_send, x_recv, own_sem,
):
    where = position()
    x, y, z, core = where
    ids = {offset: member(y, z, core, *offset) for offset in ORDER}
    me = ids[0, 0]
    other = 1 - core

    barrier = pltpu.get_barrier_semaphore()
    greeted = [(x, member(y, z, core, da, db)) for da, db in ((1, 0), (3, 0), (0, 1), (0, 3))]
    greeted += [(x, member(y, z, other, 0, 0))]
    greeted += [(lax.rem(x + dx, N_GRP), me) for dx in (1, 2, 3)]
    for device in greeted:
        pl.semaphore_signal(barrier, inc=1, device_id=device, device_id_type=MESH)

    fetches = [
        pltpu.make_async_copy(source, target, in_sem.at[i])
        for i, (source, target) in enumerate(
            ((centroids, centre_in), (owners, owners_in), (slots, slots_in), (boundary, rows_in), (vectors, residual))
        )
    ]
    for fetch in fetches:
        fetch.start()

    s_bnd = Stream(bnd, bnd_send, bnd_recv, bnd_core, where, ids)
    s_cen = Stream(cen, cen_send, cen_recv, cen_core, where, ids)

    fetches[0].wait()
    own = centre_in[...]
    cen[me] = own.astype(jnp.bfloat16)
    pl.semaphore_wait(barrier, len(greeted))

    fetches[1].wait()
    fetches[2].wait()
    owner = jnp.concatenate([owners_in[...]] * 2, axis=1)
    slot = jnp.concatenate([slots_in[...]] * 2, axis=1)
    device_row = lax.broadcasted_iota(jnp.int32, (DEVICES, 128), 0)
    named = [device_row == owner[k : k + 1, :] for k in range(LIST)]
    marks = sum(jnp.where(n, 1.0, 0.0) for n in named)
    before = lax.broadcasted_iota(jnp.int32, (128, 128), 0)
    column = lax.broadcasted_iota(jnp.int32, (128, 128), 1)
    earlier = jnp.where(before < column % BROWS, 1.0, 0.0).astype(jnp.bfloat16)
    counts = jnp.dot(marks.astype(jnp.bfloat16), earlier, preferred_element_type=jnp.float32)
    places = jnp.concatenate(
        [jnp.sum(jnp.where(n, counts, 0.0), axis=0, keepdims=True) for n in named], axis=0
    )
    lane = lax.broadcasted_iota(jnp.int32, (LIST, 128), 1)
    lists = [
        jnp.where(lane // BROWS == core, a, 0.0)
        for a in (owner.astype(jnp.float32), places, (slot + 1).astype(jnp.float32))
    ]
    squares = own * own
    partial = sum(squares[:, i * 128 : (i + 1) * 128] for i in range(D // 128))
    norms = [jnp.sum(partial[i * 128 : (i + 1) * 128].T, axis=0, keepdims=True) for i in range(2)]
    norm = jnp.concatenate(norms, axis=0) * FACTOR
    high = norm.astype(jnp.bfloat16).astype(jnp.float32)
    middle = (norm - high).astype(jnp.bfloat16).astype(jnp.float32)
    low = norm - high - middle
    info = [*lists, high, middle, low, jnp.zeros((BROWS - 3 * LIST - 6, 128), jnp.float32)]
    bnd[me, :, D:WIDE] = jnp.concatenate(info, axis=0).astype(jnp.bfloat16)
    fetches[3].wait()
    bnd[me, :, 0:D] = rows_in[...].astype(jnp.bfloat16)

    s_bnd.pass_on(0)

    fetches[4].wait()

    @pl.loop(0, V_DEV // 128)
    def _(t):
        rows = pl.ds(pl.multiple_of(t * 128, 128), 128)
        vec_bf[rows, :] = residual[rows, :].astype(jnp.bfloat16)

    srow = lax.broadcasted_iota(jnp.int32, (N_GRP * 16, 128), 0)
    scol = lax.broadcasted_iota(jnp.int32, (N_GRP * 16, 128), 1)
    wanted = ((srow // 16) * N_MEM + me) * CAP + srow % CAP
    wanted = jnp.where((srow // CAP) % 2 == scol // BROWS, wanted * FIELD, -(1 << 22))
    wanted = wanted.astype(jnp.float32)
    ones = jnp.ones((128, 128), jnp.bfloat16)

    place = lax.broadcasted_iota(jnp.int32, (N_GRP * 16, 128), 1)

    def select(e):
        da, db = ORDER[e]
        p = lax.div(ids[da, db], 2)
        s_bnd.await_core(PLACE[db, da], 2 * p + other)
        info = bnd[2 * p, 0:32, D:WIDE].astype(jnp.float32) + bnd[2 * p + 1, 0:32, D:WIDE].astype(jnp.float32)
        both = (info[0:8] * CAP + info[8:16]) * FIELD + info[16:24]
        found = jnp.zeros((N_GRP * 16, 128), jnp.float32)
        for k in range(LIST):
            apart = both[k : k + 1, :] - wanted
            found += jnp.where((apart > 0.0) & (apart < FIELD), apart, 0.0)
        pick = jnp.where(found > 0.0, 1.0, 0.0).astype(jnp.bfloat16)
        source = bnd[pl.ds(2 * p, 2), :, 0:D].reshape(128, D)
        rows = jnp.dot(pick, source, preferred_element_type=jnp.float32).astype(jnp.bfloat16)
        for g in range(N_GRP):
            parts[g, p] = rows[g * 16 : (g + 1) * 16]
        for dx in (2, 1, 3):
            pltpu.make_async_remote_copy(
                src_ref=parts.at[lax.rem(x + dx, N_GRP), p],
                dst_ref=arrived.at[x, p],
                send_sem=x_send.at[dx, 0],
                recv_sem=x_recv.at[dx, 0],
                device_id=(lax.rem(x + dx, N_GRP), me),
                device_id_type=MESH,
            ).start()
        number = jnp.dot(found.astype(jnp.bfloat16), ones, preferred_element_type=jnp.float32)
        kept[...] += jnp.where(place == p, number, 0.0)

    kept[...] = jnp.zeros_like(kept)
    for step in range(CHIPS):
        if 0 < step < CHIPS:
            s_bnd.await_block(step)
            s_bnd.pass_on(step)
        for axis, half, at in OWN_AT:
            if step == at:
                s_cen.pass_on(0, (axis,), (half,))
    def across(dx, i, arriving):
        to = lax.rem(x + dx, N_GRP)
        origin = lax.rem(x - dx + N_GRP, N_GRP) if arriving else x
        a, b = ((parts, arrived), (part_slots, arrived_slots))[i]
        return pltpu.make_async_remote_copy(
            src_ref=a.at[to],
            dst_ref=b.at[origin],
            send_sem=x_send.at[dx, i],
            recv_sem=x_recv.at[dx, i],
            device_id=(to, me),
            device_id_type=MESH,
        )

    keeps = [
        pltpu.make_async_copy(a.at[x], b.at[x], own_sem.at[i])
        for i, (a, b) in enumerate(((parts, arrived), (part_slots, arrived_slots)))
    ]

    def selected():
        for g in range(N_GRP):
            part_slots[g] = kept[g * 16 : (g + 1) * 16].astype(jnp.bfloat16)
        for dx in (2, 1, 3):
            across(dx, 1, False).start()
        for keep in keeps:
            keep.start()

    def residuals():
        for dx in (1, 2, 3):
            for i in (0, 1):
                across(dx, i, True).wait_recv()
        for keep in keeps:
            keep.wait()
        own = centre_in[...]
        high = own.astype(jnp.bfloat16)
        rest = own - high.astype(jnp.float32)
        middle = rest.astype(jnp.bfloat16)
        low = (rest - middle.astype(jnp.float32)).astype(jnp.bfloat16)
        lane = lax.broadcasted_iota(jnp.int32, (256, 128), 1)
        pair = lax.broadcasted_iota(jnp.int32, (256, 128), 0) // 16
        at = lane.astype(jnp.float32)
        for g in range(N_GRP):
            numbers = jnp.concatenate([arrived_slots[g].astype(jnp.float32)] * CHIPS, axis=0)
            numbers = jnp.where(lane == pair, numbers, 0.0).astype(jnp.bfloat16)
            number = jnp.dot(numbers, ones, preferred_element_type=jnp.float32)
            pick = jnp.concatenate(
                [jnp.where(number == at + 1.0, 1.0, 0.0), jnp.where(number == at + 129.0, 1.0, 0.0)], axis=1
            ).astype(jnp.bfloat16)
            centre = jnp.dot(pick, high, preferred_element_type=jnp.float32) + (
                jnp.dot(pick, middle, preferred_element_type=jnp.float32)
                + jnp.dot(pick, low, preferred_element_type=jnp.float32)
            )
            value = arrived[g].reshape(256, D).astype(jnp.float32) - centre
            residual[g * 256 : (g + 1) * 256, :] = value
            squares = value * value
            partial = sum(squares[:, i * 128 : (i + 1) * 128] for i in range(D // 128))
            for i in range(2):
                total = jnp.sum(partial[i * 128 : (i + 1) * 128].T, axis=0, keepdims=True)
                dist[:, (2 * g + i) * 128 : (2 * g + i + 1) * 128] = total / D

    def score(block):
        norm = norm_row(bnd, block)

        @pl.loop(0, V_DEV // TILE)
        def _(t):
            rows = pl.ds(pl.multiple_of(t * TILE, TILE), TILE)
            scores[block, rows, :] = scores_of(vec_bf[rows, :], cen[block], norm)

    @pl.loop(0, CHIPS + LAG)
    def _(i):
        for e in range(1, CHIPS):

            @pl.when(i == e)
            def _(e=e):
                s_cen.await_block(e)
                s_cen.pass_on(e)

        for n, e in enumerate(sorted(range(CHIPS), key=known)):

            @pl.when(i == 0 + n // 4)
            def _(e=e):
                select(e)

        @pl.when(i == 0 + (CHIPS - 1) // 4)
        def _():
            selected()

        @pl.when(i == RESIDUALS_AT)
        def _():
            residuals()

        @pl.when(i < CHIPS - LATER)
        def _():
            da, db = offsets(i)
            score(member(y, z, core, da, db))

        @pl.when(i >= LAG)
        def _():
            e = i - LAG
            da, db = offsets(e)
            block = member(y, z, other, da, db)
            s_cen.await_core(e, block)

            @pl.when(e < CHIPS - LATER)
            def _():
                score(block)

    for dx in (1, 2, 3):
        for i in (0, 1):
            across(dx, i, False).wait_send()
    s_bnd.await_sends()
    s_cen.await_sends()


def finish_kernel(
    scores, cen, bnd, vec_bf, residual, dist,
    scores_out, residual_out, dist_out,
    late,
    done_sem, late_sem, residual_sem,
):
    x, y, z, core = position()

    def block_of(e, side):
        da, db = offsets(e)
        return member(y, z, lax.rem(core + side, 2), da, db)

    def columns(block):
        return scores_out.at[:, pl.ds(pl.multiple_of(block * CEN, CEN), CEN)]

    def early(i):
        block = block_of(i // 2, i % 2)
        return pltpu.make_async_copy(scores.at[block], columns(block), done_sem.at[i])

    n_early, n_late = 2 * (CHIPS - LATER), 2 * LATER

    @pl.loop(0, n_early)
    def _(i):
        early(i).start()

    rows_copies = [
        pltpu.make_async_copy(residual, residual_out, residual_sem.at[0]),
        pltpu.make_async_copy(dist, dist_out, residual_sem.at[1]),
    ]
    for copy in rows_copies:
        copy.start()

    def late_copy(i):
        block = block_of(CHIPS - LATER + i // 2, i % 2)
        return pltpu.make_async_copy(late.at[i], columns(block), late_sem.at[i])

    @pl.loop(0, n_late)
    def _(i):
        block = block_of(CHIPS - LATER + i // 2, i % 2)
        norm = norm_row(bnd, block)

        @pl.loop(0, V_DEV // TILE)
        def _(t):
            rows = pl.ds(pl.multiple_of(t * TILE, TILE), TILE)
            late[i, rows, :] = scores_of(vec_bf[rows, :], cen[block], norm)

        late_copy(i).start()

    @pl.loop(0, n_early)
    def _(i):
        early(i).wait()

    @pl.loop(0, n_late)
    def _(i):
        late_copy(i).wait()

    for copy in rows_copies:
        copy.wait()


def on_device(vectors, boundary, centroids, list_owner, list_slot):
    vmem = pl.BlockSpec(memory_space=pltpu.VMEM)
    hbm = pl.BlockSpec(memory_space=pltpu.HBM)
    dma = pltpu.SemaphoreType.DMA
    stream = [dma((N_SENDS,)), dma((CHIPS, 2)), dma((CHIPS,))]
    arrays = (vectors, boundary, centroids, list_owner.T, list_slot.T)
    scores, cen, bnd, vec_bf, residual, dist = pl.pallas_call(
        gather_kernel,
        out_shape=(
            pltpu.VMEM((N_MEM, V_DEV, CEN), jnp.bfloat16),
            pltpu.VMEM((N_MEM, CEN, D), jnp.bfloat16),
            pltpu.VMEM((N_MEM, BROWS, WIDE), jnp.bfloat16),
            pltpu.VMEM((V_DEV, D), jnp.bfloat16),
            pltpu.VMEM((V_DEV, D), jnp.float32),
            pltpu.VMEM((1, DEVICES * CAP), jnp.float32),
        ),
        in_specs=[hbm] * 5,
        out_specs=[vmem] * 6,
        scratch_shapes=[
            pltpu.VMEM((N_GRP, CHIPS, 16, D), jnp.bfloat16),
            pltpu.VMEM((N_GRP, CHIPS, 16, D), jnp.bfloat16),
            pltpu.VMEM((N_GRP * 16, 128), jnp.float32),
            pltpu.VMEM((N_GRP, 16, 128), jnp.bfloat16),
            pltpu.VMEM((N_GRP, 16, 128), jnp.bfloat16),
            pltpu.VMEM((BROWS, D), jnp.float32),
            pltpu.VMEM((CEN, D), jnp.float32),
            pltpu.VMEM((LIST, BROWS), jnp.int32),
            pltpu.VMEM((LIST, BROWS), jnp.int32),
            dma((5,)),
            *stream,
            *stream,
            dma((N_GRP, 2)),
            dma((N_GRP, 2)),
            dma((2,)),
        ],
        compiler_params=pltpu.CompilerParams(
            collective_id=0, has_side_effects=True, vmem_limit_bytes=10 << 20
        ),
        name="gather",
    )(*[pltpu.with_memory_space_constraint(a, pltpu.HBM) for a in arrays])
    return pl.pallas_call(
        finish_kernel,
        out_shape=(
            jax.ShapeDtypeStruct((V_DEV, N_MEM * CEN), jnp.bfloat16),
            jax.ShapeDtypeStruct((DEVICES * CAP, D), jnp.float32),
            jax.ShapeDtypeStruct((1, DEVICES * CAP), jnp.float32),
        ),
        in_specs=[vmem] * 6,
        out_specs=[hbm] * 3,
        scratch_shapes=[
            pltpu.VMEM((2 * LATER, V_DEV, CEN), jnp.bfloat16),
            dma((2 * (CHIPS - LATER),)),
            dma((2 * LATER,)),
            dma((2,)),
        ],
        compiler_params=pltpu.CompilerParams(vmem_limit_bytes=10 << 20),
        name="finish",
    )(scores, cen, bnd, vec_bf, residual, dist)


def solution(mesh):
    spec = P(("grp", "mem"), None)
    return jax.shard_map(
        on_device,
        mesh=mesh,
        in_specs=(spec,) * 5,
        out_specs=(spec,) * 3,
        check_vma=False,
    )
```

```python
import functools
import math

import jax
import jax.numpy as jnp
from jax import lax
from jax.experimental import pallas as pl
from jax.experimental.pallas import tpu as pltpu
from jax.sharding import PartitionSpec as P

D = 768
LIST = 8
CAP = 8
BROWS = 64
WIDE = D + 128
CEN = 256
V_DEV = 1024
N_GRP = 4
N_MEM = 32
RING = 4
CHIPS = 16
DEVICES = 128
FIELD = 512
MESH = pl.DeviceIdType.MESH
FACTOR = 1.0 / math.sqrt(D)
OWN_AT = (("a", 0, 4), ("a", 1, 7), ("b", 0, 10), ("b", 1, 13), ("core", None, 13))
ROWS_LAG = 2
LATER = 4
LAG = 2
RESIDUALS_AT = 13

ORDER = (
    (0, 0), (3, 0), (1, 0), (0, 3), (0, 1), (2, 0), (3, 3), (3, 1),
    (1, 3), (1, 1), (0, 2), (2, 3), (2, 1), (3, 2), (1, 2), (2, 2),
)
PLACE = {offset: e for e, offset in enumerate(ORDER)}


def known(e):
    da, db = ORDER[e]
    return max(e, PLACE[db, da])


def sends_of(e):
    da, db = ORDER[e]
    out = []
    if db == 0:
        if da == 0:
            out += [("a", 1, h, PLACE[3, 0]) for h in (0, 1)] + [("a", 3, h, PLACE[1, 0]) for h in (0, 1)]
        elif da == 3:
            out += [("a", 1, 0, PLACE[2, 0])]
        elif da == 1:
            out += [("a", 3, 1, PLACE[2, 0])]
        for half in (0, 1) if da == 0 else (None,):
            out += [("b", 1, half, PLACE[da, 3]), ("b", 3, half, PLACE[da, 1])]
    elif db == 3:
        out += [("b", 1, 0, PLACE[da, 2])]
    elif db == 1:
        out += [("b", 3, 1, PLACE[da, 2])]
    return out + [("core", 0, None, e)]


SENDS = [sends_of(e) for e in range(CHIPS)]
FIRST = [sum(len(s) for s in SENDS[:e]) for e in range(CHIPS)]
N_SENDS = sum(len(s) for s in SENDS)


def split(order):
    da, db = ORDER[order]
    return db == 2 or (db == 0 and da == 2) or 0 in (da, db) and 2 not in (da, db)


def position():
    m = lax.axis_index("mem")
    return lax.axis_index("grp"), lax.div(m, 8), lax.rem(lax.div(m, 2), RING), lax.rem(m, 2)


def member(y, z, core, da, db):
    dy = (1 - core) * da + core * db
    dz = (1 - core) * db + core * da
    return (lax.rem(y + dy, RING) * RING + lax.rem(z + dz, RING)) * 2 + core


def offsets(e):
    da = sum(jnp.where(e == k, o[0], 0) for k, o in enumerate(ORDER))
    db = sum(jnp.where(e == k, o[1], 0) for k, o in enumerate(ORDER))
    return da, db


class Stream:
    def __init__(self, buffer, send, recv, recv_core, where, ids):
        self.buffer = buffer
        self.send, self.recv, self.recv_core = send, recv, recv_core
        self.x, self.y, self.z, self.core = where
        self.ids = ids

    def block(self, e, half):
        ref = self.buffer.at[self.ids[ORDER[e]]]
        if half is None:
            return ref
        rows = self.buffer.shape[1] // 2
        return ref.at[pl.ds(half * rows, rows)]

    def copies(self, e, axes=("a", "b", "core"), halves=(None, 0, 1)):
        out = []
        for i, (axis, step, half, there) in enumerate(SENDS[e]):
            if axis not in axes or half not in halves:
                continue
            if axis == "core":
                target, sem = self.ids[0, 0] + 1 - 2 * self.core, self.recv_core.at[e]
            else:
                target = self.ids[(step, 0) if axis == "a" else (0, step)]
                sem = self.recv.at[there, half or 0]
            ref = self.block(e, half)
            copy = pltpu.make_async_remote_copy(
                src_ref=ref,
                dst_ref=ref,
                send_sem=self.send.at[FIRST[e] + i],
                recv_sem=sem,
                device_id=(self.x, target),
                device_id_type=MESH,
            )
            out.append(copy)
        return out

    def await_block(self, e):
        if e == 0:
            return
        for half in (0, 1) if split(e) else (None,):
            ref = self.block(e, half)
            pltpu.make_async_remote_copy(
                src_ref=ref,
                dst_ref=ref,
                send_sem=self.send.at[0],
                recv_sem=self.recv.at[e, half or 0],
                device_id=(self.x, self.ids[0, 1]),
                device_id_type=MESH,
            ).wait_recv()

    def await_core(self, e, block):
        ref = self.buffer.at[block]
        pltpu.make_async_remote_copy(
            src_ref=ref,
            dst_ref=ref,
            send_sem=self.send.at[0],
            recv_sem=self.recv_core.at[e],
            device_id=(self.x, self.ids[0, 0] + 1 - 2 * self.core),
            device_id_type=MESH,
        ).wait_recv()

    def pass_on(self, e, axes=("a", "b", "core"), halves=(None, 0, 1)):
        for copy in self.copies(e, axes, halves):
            copy.start()

    def await_sends(self):
        for e in range(CHIPS):
            for copy in self.copies(e):
                copy.wait_send()


def norm_row(bnd, block):
    part = bnd[block, 16:32, D:WIDE].astype(jnp.float32)
    both = part[8:10] + (part[10:12] + part[12:14])
    return jnp.concatenate([both[0:1], both[1:2]], axis=1)


def scores_of(vec, rows, norm):
    products = lax.dot_general(
        vec, rows, (((1,), (1,)), ((), ())), preferred_element_type=jnp.float32
    )
    return (products * (2.0 * FACTOR) - norm).astype(jnp.bfloat16)


TILE = 1024


def gather_kernel(
    vectors, boundary, centroids, owners, slots,
    scores, cen, bnd, vec_bf, residual, dist,
    parts, arrived, kept, part_slots, arrived_slots, rows_in, centre_in, owners_in, slots_in,
    in_sem,
    bnd_send, bnd_recv, bnd_core,
    cen_send, cen_recv, cen_core,
    x_send, x_recv, own_sem,
):
    where = position()
    x, y, z, core = where
    ids = {offset: member(y, z, core, *offset) for offset in ORDER}
    me = ids[0, 0]
    other = 1 - core

    barrier = pltpu.get_barrier_semaphore()
    greeted = [(x, member(y, z, core, da, db)) for da, db in ((1, 0), (3, 0), (0, 1), (0, 3))]
    greeted += [(x, member(y, z, other, 0, 0))]
    greeted += [(lax.rem(x + dx, N_GRP), me) for dx in (1, 2, 3)]
    for device in greeted:
        pl.semaphore_signal(barrier, inc=1, device_id=device, device_id_type=MESH)

    fetches = [
        pltpu.make_async_copy(source, target, in_sem.at[i])
        for i, (source, target) in enumerate(
            ((centroids, centre_in), (owners, owners_in), (slots, slots_in), (boundary, rows_in), (vectors, residual))
        )
    ]
    for fetch in fetches:
        fetch.start()

    s_bnd = Stream(bnd, bnd_send, bnd_recv, bnd_core, where, ids)
    s_cen = Stream(cen, cen_send, cen_recv, cen_core, where, ids)

    fetches[0].wait()
    own = centre_in[...]
    cen[me] = own.astype(jnp.bfloat16)

    fetches[1].wait()
    fetches[2].wait()
    owner = jnp.concatenate([owners_in[...]] * 2, axis=1)
    slot = jnp.concatenate([slots_in[...]] * 2, axis=1)
    device_row = lax.broadcasted_iota(jnp.int32, (DEVICES, 128), 0)
    named = [device_row == owner[k : k + 1, :] for k in range(LIST)]
    marks = sum(jnp.where(n, 1.0, 0.0) for n in named)
    before = lax.broadcasted_iota(jnp.int32, (128, 128), 0)
    column = lax.broadcasted_iota(jnp.int32, (128, 128), 1)
    earlier = jnp.where(before < column % BROWS, 1.0, 0.0).astype(jnp.bfloat16)
    counts = jnp.dot(marks.astype(jnp.bfloat16), earlier, preferred_element_type=jnp.float32)
    places = jnp.concatenate(
        [jnp.sum(jnp.where(n, counts, 0.0), axis=0, keepdims=True) for n in named], axis=0
    )
    lane = lax.broadcasted_iota(jnp.int32, (LIST, 128), 1)
    lists = [
        jnp.where(lane // BROWS == core, a, 0.0)
        for a in (owner.astype(jnp.float32), places, (slot + 1).astype(jnp.float32))
    ]
    squares = own * own
    partial = sum(squares[:, i * 128 : (i + 1) * 128] for i in range(D // 128))
    norms = [jnp.sum(partial[i * 128 : (i + 1) * 128].T, axis=0, keepdims=True) for i in range(2)]
    norm = jnp.concatenate(norms, axis=0) * FACTOR
    high = norm.astype(jnp.bfloat16).astype(jnp.float32)
    middle = (norm - high).astype(jnp.bfloat16).astype(jnp.float32)
    low = norm - high - middle
    info = [*lists, high, middle, low, jnp.zeros((BROWS - 3 * LIST - 6, 128), jnp.float32)]
    bnd[me, :, D:WIDE] = jnp.concatenate(info, axis=0).astype(jnp.bfloat16)
    fetches[3].wait()
    bnd[me, :, 0:D] = rows_in[...].astype(jnp.bfloat16)

    pl.semaphore_wait(barrier, len(greeted))
    s_bnd.pass_on(0)

    fetches[4].wait()

    @pl.loop(0, V_DEV // 128)
    def _(t):
        rows = pl.ds(pl.multiple_of(t * 128, 128), 128)
        vec_bf[rows, :] = residual[rows, :].astype(jnp.bfloat16)

    srow = lax.broadcasted_iota(jnp.int32, (N_GRP * 16, 128), 0)
    scol = lax.broadcasted_iota(jnp.int32, (N_GRP * 16, 128), 1)
    wanted = ((srow // 16) * N_MEM + me) * CAP + srow % CAP
    wanted = jnp.where((srow // CAP) % 2 == scol // BROWS, wanted * FIELD, -(1 << 22))
    wanted = wanted.astype(jnp.float32)
    ones = jnp.ones((128, 128), jnp.bfloat16)

    place = lax.broadcasted_iota(jnp.int32, (N_GRP * 16, 128), 1)

    def select(e):
        da, db = ORDER[e]
        p = lax.div(ids[da, db], 2)
        s_bnd.await_core(PLACE[db, da], 2 * p + other)
        info = bnd[2 * p, 0:32, D:WIDE].astype(jnp.float32) + bnd[2 * p + 1, 0:32, D:WIDE].astype(jnp.float32)
        both = (info[0:8] * CAP + info[8:16]) * FIELD + info[16:24]
        found = jnp.zeros((N_GRP * 16, 128), jnp.float32)
        for k in range(LIST):
            apart = both[k : k + 1, :] - wanted
            found += jnp.where((apart > 0.0) & (apart < FIELD), apart, 0.0)
        pick = jnp.where(found > 0.0, 1.0, 0.0).astype(jnp.bfloat16)
        source = bnd[pl.ds(2 * p, 2), :, 0:D].reshape(128, D)
        rows = jnp.dot(pick, source, preferred_element_type=jnp.float32).astype(jnp.bfloat16)
        for g in range(N_GRP):
            parts[g, p] = rows[g * 16 : (g + 1) * 16]
        for dx in (2, 1, 3):
            pltpu.make_async_remote_copy(
                src_ref=parts.at[lax.rem(x + dx, N_GRP), p],
                dst_ref=arrived.at[x, p],
                send_sem=x_send.at[dx, 0],
                recv_sem=x_recv.at[dx, 0],
                device_id=(lax.rem(x + dx, N_GRP), me),
                device_id_type=MESH,
            ).start()
        number = jnp.dot(found.astype(jnp.bfloat16), ones, preferred_element_type=jnp.float32)
        kept[...] += jnp.where(place == p, number, 0.0)

    kept[...] = jnp.zeros_like(kept)
    for step in range(CHIPS):
        if 0 < step < CHIPS:
            s_bnd.await_block(step)
            s_bnd.pass_on(step)
        for axis, half, at in OWN_AT:
            if step == at:
                s_cen.pass_on(0, (axis,), (half,))
    def across(dx, i, arriving):
        to = lax.rem(x + dx, N_GRP)
        origin = lax.rem(x - dx + N_GRP, N_GRP) if arriving else x
        a, b = ((parts, arrived), (part_slots, arrived_slots))[i]
        return pltpu.make_async_remote_copy(
            src_ref=a.at[to],
            dst_ref=b.at[origin],
            send_sem=x_send.at[dx, i],
            recv_sem=x_recv.at[dx, i],
            device_id=(to, me),
            device_id_type=MESH,
        )

    keeps = [
        pltpu.make_async_copy(a.at[x], b.at[x], own_sem.at[i])
        for i, (a, b) in enumerate(((parts, arrived), (part_slots, arrived_slots)))
    ]

    def selected():
        for g in range(N_GRP):
            part_slots[g] = kept[g * 16 : (g + 1) * 16].astype(jnp.bfloat16)
        for dx in (2, 1, 3):
            across(dx, 1, False).start()
        for keep in keeps:
            keep.start()

    def residuals():
        for dx in (1, 2, 3):
            for i in (0, 1):
                across(dx, i, True).wait_recv()
        for keep in keeps:
            keep.wait()
        own = centre_in[...]
        high = own.astype(jnp.bfloat16)
        rest = own - high.astype(jnp.float32)
        middle = rest.astype(jnp.bfloat16)
        low = (rest - middle.astype(jnp.float32)).astype(jnp.bfloat16)
        lane = lax.broadcasted_iota(jnp.int32, (256, 128), 1)
        pair = lax.broadcasted_iota(jnp.int32, (256, 128), 0) // 16
        at = lane.astype(jnp.float32)
        for g in range(N_GRP):
            numbers = jnp.concatenate([arrived_slots[g].astype(jnp.float32)] * CHIPS, axis=0)
            numbers = jnp.where(lane == pair, numbers, 0.0).astype(jnp.bfloat16)
            number = jnp.dot(numbers, ones, preferred_element_type=jnp.float32)
            pick = jnp.concatenate(
                [jnp.where(number == at + 1.0, 1.0, 0.0), jnp.where(number == at + 129.0, 1.0, 0.0)], axis=1
            ).astype(jnp.bfloat16)
            centre = jnp.dot(pick, high, preferred_element_type=jnp.float32) + (
                jnp.dot(pick, middle, preferred_element_type=jnp.float32)
                + jnp.dot(pick, low, preferred_element_type=jnp.float32)
            )
            value = arrived[g].reshape(256, D).astype(jnp.float32) - centre
            residual[g * 256 : (g + 1) * 256, :] = value
            squares = value * value
            partial = sum(squares[:, i * 128 : (i + 1) * 128] for i in range(D // 128))
            for i in range(2):
                total = jnp.sum(partial[i * 128 : (i + 1) * 128].T, axis=0, keepdims=True)
                dist[:, (2 * g + i) * 128 : (2 * g + i + 1) * 128] = total / D

    def score(block):
        norm = norm_row(bnd, block)

        @pl.loop(0, V_DEV // TILE)
        def _(t):
            rows = pl.ds(pl.multiple_of(t * TILE, TILE), TILE)
            scores[block, rows, :] = scores_of(vec_bf[rows, :], cen[block], norm)

    @pl.loop(0, CHIPS + LAG)
    def _(i):
        for e in range(1, CHIPS):

            @pl.when(i == e)
            def _(e=e):
                s_cen.await_block(e)
                s_cen.pass_on(e)

        for n, e in enumerate(sorted(range(CHIPS), key=known)):

            @pl.when(i == 0 + n // 4)
            def _(e=e):
                select(e)

        @pl.when(i == 0 + (CHIPS - 1) // 4)
        def _():
            selected()

        @pl.when(i == RESIDUALS_AT)
        def _():
            residuals()

        @pl.when(i < CHIPS - LATER)
        def _():
            da, db = offsets(i)
            score(member(y, z, core, da, db))

        @pl.when(i >= LAG)
        def _():
            e = i - LAG
            da, db = offsets(e)
            block = member(y, z, other, da, db)
            s_cen.await_core(e, block)

            @pl.when(e < CHIPS - LATER)
            def _():
                score(block)

    for dx in (1, 2, 3):
        for i in (0, 1):
            across(dx, i, False).wait_send()
    s_bnd.await_sends()
    s_cen.await_sends()


def finish_kernel(
    scores, cen, bnd, vec_bf, residual, dist,
    scores_out, residual_out, dist_out,
    late,
    done_sem, late_sem, residual_sem,
):
    x, y, z, core = position()

    def block_of(e, side):
        da, db = offsets(e)
        return member(y, z, lax.rem(core + side, 2), da, db)

    def columns(block):
        return scores_out.at[:, pl.ds(pl.multiple_of(block * CEN, CEN), CEN)]

    def early(i):
        block = block_of(i // 2, i % 2)
        return pltpu.make_async_copy(scores.at[block], columns(block), done_sem.at[i])

    n_early, n_late = 2 * (CHIPS - LATER), 2 * LATER

    @pl.loop(0, n_early)
    def _(i):
        early(i).start()

    rows_copies = [
        pltpu.make_async_copy(residual, residual_out, residual_sem.at[0]),
        pltpu.make_async_copy(dist, dist_out, residual_sem.at[1]),
    ]
    for copy in rows_copies:
        copy.start()

    def late_copy(i):
        block = block_of(CHIPS - LATER + i // 2, i % 2)
        return pltpu.make_async_copy(late.at[i], columns(block), late_sem.at[i])

    @pl.loop(0, n_late)
    def _(i):
        block = block_of(CHIPS - LATER + i // 2, i % 2)
        norm = norm_row(bnd, block)

        @pl.loop(0, V_DEV // TILE)
        def _(t):
            rows = pl.ds(pl.multiple_of(t * TILE, TILE), TILE)
            late[i, rows, :] = scores_of(vec_bf[rows, :], cen[block], norm)

        late_copy(i).start()

    @pl.loop(0, n_early)
    def _(i):
        early(i).wait()

    @pl.loop(0, n_late)
    def _(i):
        late_copy(i).wait()

    for copy in rows_copies:
        copy.wait()


def on_device(vectors, boundary, centroids, list_owner, list_slot):
    vmem = pl.BlockSpec(memory_space=pltpu.VMEM)
    hbm = pl.BlockSpec(memory_space=pltpu.HBM)
    dma = pltpu.SemaphoreType.DMA
    stream = [dma((N_SENDS,)), dma((CHIPS, 2)), dma((CHIPS,))]
    arrays = (vectors, boundary, centroids, list_owner.T, list_slot.T)
    scores, cen, bnd, vec_bf, residual, dist = pl.pallas_call(
        gather_kernel,
        out_shape=(
            pltpu.VMEM((N_MEM, V_DEV, CEN), jnp.bfloat16),
            pltpu.VMEM((N_MEM, CEN, D), jnp.bfloat16),
            pltpu.VMEM((N_MEM, BROWS, WIDE), jnp.bfloat16),
            pltpu.VMEM((V_DEV, D), jnp.bfloat16),
            pltpu.VMEM((V_DEV, D), jnp.float32),
            pltpu.VMEM((1, DEVICES * CAP), jnp.float32),
        ),
        in_specs=[hbm] * 5,
        out_specs=[vmem] * 6,
        scratch_shapes=[
            pltpu.VMEM((N_GRP, CHIPS, 16, D), jnp.bfloat16),
            pltpu.VMEM((N_GRP, CHIPS, 16, D), jnp.bfloat16),
            pltpu.VMEM((N_GRP * 16, 128), jnp.float32),
            pltpu.VMEM((N_GRP, 16, 128), jnp.bfloat16),
            pltpu.VMEM((N_GRP, 16, 128), jnp.bfloat16),
            pltpu.VMEM((BROWS, D), jnp.float32),
            pltpu.VMEM((CEN, D), jnp.float32),
            pltpu.VMEM((LIST, BROWS), jnp.int32),
            pltpu.VMEM((LIST, BROWS), jnp.int32),
            dma((5,)),
            *stream,
            *stream,
            dma((N_GRP, 2)),
            dma((N_GRP, 2)),
            dma((2,)),
        ],
        compiler_params=pltpu.CompilerParams(
            collective_id=0, has_side_effects=True, vmem_limit_bytes=10 << 20
        ),
        name="gather",
    )(*[pltpu.with_memory_space_constraint(a, pltpu.HBM) for a in arrays])
    return pl.pallas_call(
        finish_kernel,
        out_shape=(
            jax.ShapeDtypeStruct((V_DEV, N_MEM * CEN), jnp.bfloat16),
            jax.ShapeDtypeStruct((DEVICES * CAP, D), jnp.float32),
            jax.ShapeDtypeStruct((1, DEVICES * CAP), jnp.float32),
        ),
        in_specs=[vmem] * 6,
        out_specs=[hbm] * 3,
        scratch_shapes=[
            pltpu.VMEM((2 * LATER, V_DEV, CEN), jnp.bfloat16),
            dma((2 * (CHIPS - LATER),)),
            dma((2 * LATER,)),
            dma((2,)),
        ],
        compiler_params=pltpu.CompilerParams(vmem_limit_bytes=10 << 20),
        name="finish",
    )(scores, cen, bnd, vec_bf, residual, dist)


def solution(mesh):
    spec = P(("grp", "mem"), None)
    return jax.shard_map(
        on_device,
        mesh=mesh,
        in_specs=(spec,) * 5,
        out_specs=(spec,) * 3,
        check_vma=False,
    )
```
